128 devices in a mesh: grid: 8 (over x, core), row: 4 (over y), col: 4 (over z).
Axes of the slice: x: 4, y: 4, z: 4, core: 2. Of those that a mesh axis runs over, the one named last changes fastest.
Arguments:
- rhs_in: bfloat16 [131072, 1024], P(('grid', 'row', 'col')), may hold values from -6 to 6
- rhs_target: int32 [131072], P(('grid', 'row', 'col')), may hold values from 0 to 131071, as said below
- leaf_inverse: bfloat16 [256, 512, 512], P(('grid', 'row', 'col')), may hold values from -0.25 to 0.25
- level_one_blocks: bfloat16 [8, 4, 4, 4, 2, 512, 512], P('grid', 'row', 'col'), may hold values from -0.0625 to 0.0625
- level_one_pattern: int32 [8, 4, 4, 4, 2], P('grid', 'row', 'col'), may hold values 0 or 1
- level_one_rhs: bfloat16 [8, 4, 512, 1024], P('grid', 'row', None, 'col'), may hold values from -6 to 6
- level_one_inverse: bfloat16 [8, 4, 512, 512], P('grid', 'row'), may hold values from -0.25 to 0.25
- top_blocks: bfloat16 [8, 4, 4, 512, 512], P('grid', 'row'), may hold values from -0.046875 to 0.046875
- top_rhs: bfloat16 [4, 512, 1024], P(None, None, 'col'), may hold values from -6 to 6
- top_inverse: bfloat16 [4, 512, 512], replicated, may hold values from -0.25 to 0.25
- top_chain: bfloat16 [6, 512, 512], replicated, may hold values from -0.125 to 0.125
Outputs:
- leaf_solution: bfloat16 [131072, 1024], P(('grid', 'row', 'col'))
- level_one_solution: bfloat16 [8, 4, 512, 1024], P('grid', 'row', None, 'col')
- top_solution: bfloat16 [4, 512, 1024], P(None, None, 'col')
The draws below stay inside these ranges and needn't reach their ends.
Inputs may be any that keep to these rules, and one draw needn't show every extreme that they name: rhs_target is a permutation; position p belongs to the device of flat index p // 1024 over grid, row, col (grid slowest); the 1024 arrival rows of every device go exactly 8 to each device.
All inputs are finite; a program needn't handle non-finite values. No bound on the sum of `level_one_pattern` on one device may be relied on, other than what follows from the above.
Results may differ from the reference program's by a relative error of at most 0.02.
Values may be sent and summed in bfloat16 or wider, within the bound.
No kernel may reach another device: no remote copies, remote signals or barrier semaphores. Data moves between devices by JAX's collectives and lax.ppermute only.
A program may use at most 128 MiB of HBM per device.

```python
import jax
import jax.numpy as jnp
from jax import lax

S = 512
R = 1024
LEAF_DEV = 2
TOPS = 4
GRIDS = 8
BROWS = 4
BCOLS = 4
ROWS_DEV = 1024
ALL_ROWS = 131072
LEAVES = 256
PAIRS = 6


def draw_rhs_target(key, part):
    device_count = ALL_ROWS // ROWS_DEV
    share_rows = ROWS_DEV // device_count
    first_key, second_key = jax.random.split(jax.random.fold_in(key, 17))
    column_ids = jnp.arange(ROWS_DEV, dtype=jnp.int32)[None, :]
    scores = jax.random.randint(first_key, (device_count, ROWS_DEV), 0, 65536) * ROWS_DEV + column_ids
    local_order = jnp.argsort(scores, axis=1).astype(jnp.int32)
    grouped = local_order.reshape(device_count, device_count, share_rows)
    owners = jnp.arange(device_count, dtype=jnp.int32)[:, None, None] * ROWS_DEV
    positions = grouped + owners
    per_source = jnp.transpose(positions, (1, 0, 2)).reshape(device_count, ROWS_DEV)
    shuffle_scores = jax.random.randint(second_key, (device_count, ROWS_DEV), 0, 65536) * ROWS_DEV + column_ids
    shuffle = jnp.argsort(shuffle_scores, axis=1)
    mixed = jnp.take_along_axis(per_source, shuffle, axis=1)
    return mixed.reshape(ALL_ROWS).astype(jnp.int32)


def set_ends(array, rng, low, high):
    place = [jax.random.randint(jax.random.fold_in(rng, axis), (), 0, length) for axis, length in enumerate(array.shape)]
    main_axis = array.shape.index(max(array.shape))
    next_to = place[:main_axis] + [(place[main_axis] + 1) % array.shape[main_axis]] + place[main_axis + 1:]
    return array.at[tuple(place)].set(low).at[tuple(next_to)].set(high)


def block_levels(own_key, extent, cuts, least, top_value):
    def one(axis_at, shards_of):
        steps = jax.random.uniform(jax.random.fold_in(jax.random.fold_in(own_key, 6), axis_at), (shards_of,), jnp.float32, least / len(cuts), top_value / len(cuts))
        return jnp.repeat(jnp.exp(steps), extent[axis_at] // shards_of).reshape((-1,) + (1,) * (len(extent) - axis_at - 1))

    level = one(*cuts[0])
    for cut in cuts[1:]:
        level = level * one(*cut)
    return level


def bell_draw(stream_key, extent, scale, limit, cuts=(), held_as=jnp.bfloat16):
    factor_of = block_levels(stream_key, extent, cuts, -0.22, 0.18) if cuts else 1.0
    array = jax.random.normal(stream_key, extent, jnp.float32) * scale * factor_of
    return jnp.minimum(jnp.maximum(array, -limit), limit).astype(held_as)


def setup_inputs(seed: int = 0) -> dict:
    splits = jax.random.split(jax.random.key(seed), 12)
    rhs_in = bell_draw(splits[0], (ALL_ROWS, R), 1.0, 6.0, ((0, 128),))
    rhs_target = draw_rhs_target(jax.random.fold_in(splits[11], 71), 0)
    leaf_inverse = bell_draw(splits[2], (LEAVES, S, S), S ** -0.5, 0.25, ((0, 128),))
    level_one_blocks = bell_draw(splits[3], (GRIDS, BROWS, BCOLS, BROWS, LEAF_DEV, S, S), (BROWS * BCOLS * LEAF_DEV * S // 2) ** -0.5, 0.0625, ((0, 8), (1, 4), (2, 4)))
    level_one_pattern = set_ends((jax.random.randint(splits[4], (GRIDS, BROWS, BCOLS, BROWS, LEAF_DEV), 0, 2) < 1).astype(jnp.int32), jax.random.fold_in(splits[4], 1), 0, 1)
    level_one_rhs = bell_draw(splits[5], (GRIDS, BROWS, S, R), 1.0, 6.0, ((0, 8), (1, 4), (3, 4)))
    level_one_inverse = bell_draw(splits[6], (GRIDS, BROWS, S, S), S ** -0.5, 0.25, ((0, 8), (1, 4)))
    top_blocks = bell_draw(splits[7], (GRIDS, BROWS, TOPS, S, S), (GRIDS * BROWS * S) ** -0.5, 0.046875, ((0, 8), (1, 4)))
    top_rhs = bell_draw(splits[8], (TOPS, S, R), 1.0, 6.0, ((2, 4),))
    top_inverse = bell_draw(splits[9], (TOPS, S, S), S ** -0.5, 0.25)
    top_chain = bell_draw(splits[10], (PAIRS, S, S), (TOPS * S) ** -0.5, 0.125)
    return {"rhs_in": rhs_in, "rhs_target": rhs_target, "leaf_inverse": leaf_inverse, "level_one_blocks": level_one_blocks, "level_one_pattern": level_one_pattern, "level_one_rhs": level_one_rhs, "level_one_inverse": level_one_inverse, "top_blocks": top_blocks, "top_rhs": top_rhs, "top_inverse": top_inverse, "top_chain": top_chain}


def leaf_solve(operands):
    inverse_block, rhs_block = operands
    return jnp.dot(inverse_block, rhs_block, preferred_element_type=jnp.float32).astype(jnp.bfloat16)


def level_one_grid(operands):
    leaf_grid, blocks, pattern, rhs_one, inverse_one = operands
    solved = leaf_grid.astype(jnp.float32)
    masked = blocks.astype(jnp.float32) * pattern.astype(jnp.float32)[..., None, None]
    update_one = jnp.einsum("kcmlij,mcljr->kir", masked, solved)
    resid_one = (rhs_one.astype(jnp.float32) - update_one).astype(jnp.bfloat16)
    return jnp.einsum("kij,kjr->kir", inverse_one.astype(jnp.float32), resid_one.astype(jnp.float32)).astype(jnp.bfloat16)


def reference(rhs_in, rhs_target, leaf_inverse, level_one_blocks, level_one_pattern, level_one_rhs, level_one_inverse, top_blocks, top_rhs, top_inverse, top_chain):
    placed = rhs_in[jnp.argsort(rhs_target)]
    leaf_rhs = placed.reshape(LEAVES, S, R)
    leaf_solution = lax.map(leaf_solve, (leaf_inverse, leaf_rhs))
    leaf_grid = leaf_solution.reshape(GRIDS, BROWS, BCOLS, LEAF_DEV, S, R)
    level_one_solution = lax.map(level_one_grid, (leaf_grid, level_one_blocks, level_one_pattern, level_one_rhs, level_one_inverse))
    top_update = jnp.einsum("gktij,gkjr->tir", top_blocks.astype(jnp.float32), level_one_solution.astype(jnp.float32))
    solved = []
    for current in range(TOPS):
        running = top_rhs[current].astype(jnp.float32) - top_update[current]
        for earlier in range(current):
            running = running - jnp.dot(top_chain[current * (current - 1) // 2 + earlier], solved[earlier], preferred_element_type=jnp.float32)
        solved.append(jnp.dot(top_inverse[current], running.astype(jnp.bfloat16), preferred_element_type=jnp.float32).astype(jnp.bfloat16))
    top_solution = jnp.stack(solved)
    return leaf_solution.reshape(ALL_ROWS, R), level_one_solution, top_solution
```

```python
import jax
import jax.numpy as jnp
from jax import lax
from jax.experimental import pallas as pl
from jax.experimental.pallas import tpu as pltpu
from jax.sharding import PartitionSpec as P

F32 = jnp.float32
BF16 = jnp.bfloat16
LANES = 128
VMEM_LIMIT = 56 * 1024 * 1024


def params():
    return pltpu.CompilerParams(vmem_limit_bytes=VMEM_LIMIT)


def mm(a, b):
    return jnp.dot(a, b, preferred_element_type=F32)


def mm_nt(a, b):
    return lax.dot_general(a, b, (((1,), (1,)), ((), ())), preferred_element_type=F32)


def pick_kernel(row_ref, pattern_ref, block_ref, far_first_ref, far_second_ref, next_ref, last_ref):
    rows, leaves = pattern_ref.shape[1], block_ref.shape[1]
    outs = ((far_first_ref, far_second_ref), (next_ref.at[0], next_ref.at[1]), (last_ref.at[0], last_ref.at[1]))
    for index, step in enumerate((2, 1, 3)):

        @pl.when(pl.program_id(0) == index)
        def _():
            for leaf in range(leaves):
                present = pattern_ref[leaf, (row_ref[0] + step) % rows].astype(F32).astype(BF16)
                outs[index][leaf][...] = block_ref[0, leaf] * present


def pick(row, pattern, blocks):
    rows, leaves, size, _ = blocks.shape

    def source(i, at, pattern):
        return ((at[0] + jnp.where(i == 0, 2, jnp.where(i == 1, 1, 3))) % rows, 0, 0, 0)

    return pl.pallas_call(
        pick_kernel,
        grid_spec=pltpu.PrefetchScalarGridSpec(
            num_scalar_prefetch=2,
            grid=(3,),
            in_specs=[pl.BlockSpec((1, leaves, size, size), source)],
            out_specs=[pl.BlockSpec((size, size), lambda i, at, pattern: (0, 0))] * 2
            + [pl.BlockSpec((leaves, size, size), lambda i, at, pattern: (0, 0, 0))] * 2,
        ),
        out_shape=[jax.ShapeDtypeStruct((size, size), BF16)] * 2
        + [jax.ShapeDtypeStruct((leaves, size, size), BF16)] * 2,
        compiler_params=params(),
        name="pick",
    )(row.reshape(1), pattern, blocks)


def route_kernel(device_count, target_ref, rows_ref, out_ref, slot_ref):
    count = target_ref.shape[1]
    share = count // device_count
    part = out_ref.shape[0]
    width = rows_ref.shape[1]
    step = pl.program_id(0)

    @pl.when(step == 0)
    def _():
        target = target_ref[...]
        owner = target // count
        place = target % count
        piece = 2 * LANES
        before = (
            lax.broadcasted_iota(jnp.int32, (piece, piece), 0)
            < lax.broadcasted_iota(jnp.int32, (piece, piece), 1)
        ).astype(BF16)
        device = lax.broadcasted_iota(jnp.int32, (device_count, piece), 0)
        base = device[:, :1].astype(F32) * share
        for first in range(0, count, piece):
            mine = (device == owner[:, first : first + piece]).astype(F32)
            rank = mm(mine.astype(BF16), before) + base
            slot_ref[0:1, first : first + piece] = jnp.sum(mine * rank, axis=0, keepdims=True)
            base = base + jnp.sum(mine, axis=1, keepdims=True)
        slot_ref[1:2, :] = (place // 32).astype(F32)
        slot_ref[2:3, :] = (place % 32).astype(F32)

    slot = slot_ref[0:1, :].astype(jnp.int32)
    rows_at = lax.broadcasted_iota(jnp.int32, (part, count), 0) + step * part
    pick = (rows_at == slot).astype(BF16)
    out_ref[:, :width] = mm(pick, rows_ref[...]).astype(BF16)
    which = lax.broadcasted_iota(jnp.int32, (LANES, count), 0)
    digits = jnp.where(which == 0, slot_ref[1:2, :], jnp.where(which == 1, slot_ref[2:3, :], 0.0))
    out_ref[:, width:] = mm_nt(pick, digits.astype(BF16)).astype(BF16)


def route(rhs_target, rhs_in, device_count):
    rows, width = rhs_in.shape
    parts = 4
    return pl.pallas_call(
        lambda *refs: route_kernel(device_count, *refs),
        grid=(parts,),
        in_specs=[
            pl.BlockSpec((1, rows), lambda i: (0, 0)),
            pl.BlockSpec((rows, width), lambda i: (0, 0)),
        ],
        out_specs=pl.BlockSpec((rows // parts, width + LANES), lambda i: (i, 0)),
        out_shape=jax.ShapeDtypeStruct((rows, width + LANES), BF16),
        scratch_shapes=[pltpu.VMEM((8, rows), F32)],
        compiler_params=params(),
        name="route",
    )(rhs_target.reshape(1, rows), rhs_in)


def leaf_kernel(digits_ref, inverse_ref, got_ref, out_ref, mixed_ref):
    leaves, size = inverse_ref.shape[0], inverse_ref.shape[1]
    rows = leaves * size

    @pl.when(pl.program_id(0) == 0)
    def _():
        lane = lax.broadcasted_iota(jnp.int32, (8, LANES), 1)
        weights = jnp.where(lane == 0, 32.0, jnp.where(lane == 1, 1.0, 0.0)).astype(BF16)
        place = mm_nt(weights, digits_ref[...])[0:1, :].astype(jnp.int32)
        for leaf in range(leaves):
            at = lax.broadcasted_iota(jnp.int32, (size, rows), 0) + leaf * size
            pick = (at == place).astype(BF16)
            mixed_ref[leaf * size : (leaf + 1) * size, :] = mm(inverse_ref[leaf], pick).astype(BF16)

    out_ref[...] = mm(mixed_ref[...], got_ref[...]).astype(BF16)


def leaf_solve(got, leaf_inverse):
    rows = got.shape[0]
    width = got.shape[1] - LANES
    leaves, size, _ = leaf_inverse.shape
    block = 256
    return pl.pallas_call(
        leaf_kernel,
        grid=(width // block,),
        in_specs=[
            pl.BlockSpec((rows, LANES), lambda i: (0, width // LANES)),
            pl.BlockSpec((leaves, size, size), lambda i: (0, 0, 0)),
            pl.BlockSpec((rows, block), lambda i: (0, i)),
        ],
        out_specs=pl.BlockSpec((rows, block), lambda i: (0, i)),
        out_shape=jax.ShapeDtypeStruct((rows, width), BF16),
        scratch_shapes=[pltpu.VMEM((rows, rows), BF16)],
        compiler_params=params(),
        name="leaf_solve",
    )(got, leaf_inverse, got)


def couple_kernel(cols, items, at_ref, pattern_ref, solved_ref, *refs):
    count, rows = sum(items), len(items)
    inputs, upper, lower = refs[:count], refs[count : count + cols], refs[count + cols :]
    size = inputs[0].shape[-1]
    half = size // 2
    for offset in range(cols):

        @pl.when(pl.program_id(0) == offset)
        def _():
            first = 0
            for index, item in enumerate(items):
                total = None
                for leaf in range(solved_ref.shape[0] // size):
                    block = inputs[first + leaf] if item > 1 else inputs[first]
                    own = len(block.shape) == 4
                    factor = block[...] if item > 1 else block[0, leaf] if own else block[leaf]
                    term = mm(factor, solved_ref[leaf * size : (leaf + 1) * size, :])
                    if own:
                        term = term * pattern_ref[leaf, at_ref[1]].astype(F32)
                    total = term if total is None else total + term
                upper[offset][index] = total[:half].astype(BF16)
                lower[index][offset] = total[half:].astype(BF16)
                first += item


def couple(col, row, cols, pattern, solved, groups):
    rows, width = solved.shape
    block = width // cols
    flat = [item for group in groups for item in group]
    size = flat[0].shape[-1]
    specs = []
    for item in flat:
        if len(item.shape) == 4:
            specs.append(pl.BlockSpec((1,) + item.shape[1:], lambda i, at, pattern: (at[1], 0, 0, 0)))
        else:
            zeros = (0,) * len(item.shape)
            specs.append(pl.BlockSpec(item.shape, lambda i, at, pattern, zeros=zeros: zeros))
    shapes = [(len(groups), size // 2, block)] * cols + [(cols, size // 2, block)] * len(groups)
    outs = pl.pallas_call(
        lambda *refs: couple_kernel(cols, [len(group) for group in groups], *refs),
        grid_spec=pltpu.PrefetchScalarGridSpec(
            num_scalar_prefetch=2,
            grid=(cols,),
            in_specs=[pl.BlockSpec((rows, block), lambda i, at, pattern: (0, (at[0] + i) % cols))] + specs,
            out_specs=[pl.BlockSpec(shape, lambda i, at, pattern: (0, 0, 0)) for shape in shapes],
        ),
        out_shape=[jax.ShapeDtypeStruct(shape, BF16) for shape in shapes],
        compiler_params=params(),
        name="couple",
    )(jnp.stack([col, row]).astype(jnp.int32), pattern, solved, *flat)
    return outs[:cols], outs[cols:]


def half_sum_kernel(count, *refs):
    for side in range(2):
        parts, outs = refs[side * count : (side + 1) * count], refs[2 * count :]
        for index in range(parts[0].shape[0]):
            total = parts[0][index].astype(F32)
            for part in parts[1:]:
                total += part[index].astype(F32)
            out = outs[side * parts[0].shape[0] + index]
            out[...] = total.astype(out.dtype)


def half_sums(upper, lower):
    shape = upper[0].shape[1:]
    outs = [
        jax.ShapeDtypeStruct(shape, F32 if index == 0 else BF16)
        for side in (upper, lower)
        for index in range(side[0].shape[0])
    ]
    sums = pl.pallas_call(
        lambda *refs: half_sum_kernel(len(upper), *refs), out_shape=outs, compiler_params=params(), name="half_sums"
    )(*upper, *lower)
    return sums[: len(sums) // 2], sums[len(sums) // 2 :]


def chain_kernel(inverse_ref, chain_ref, blocks_ref, rhs_ref, mixed_ref, chained_ref, solved_ref):
    tops, size = inverse_ref.shape[0], inverse_ref.shape[1]
    for now in range(tops):
        left = blocks_ref[now].astype(F32)
        right = rhs_ref[now].astype(F32)
        for earlier in range(now):
            link = chain_ref[now * (now - 1) // 2 + earlier]
            at = slice(earlier * size, (earlier + 1) * size)
            left = left - mm(link, mixed_ref[at, :])
            right = right - mm(link, solved_ref[at, :])
        inverse = inverse_ref[now]
        at = slice(now * size, (now + 1) * size)
        mixed_ref[at, :] = mm(inverse, left.astype(BF16)).astype(BF16)
        answer = mm(inverse, right.astype(BF16))
        solved_ref[at, :] = answer.astype(BF16)
        chained_ref[at, :] = answer


def chain_blocks(top_inverse, top_chain, top_blocks, top_rhs):
    tops, size, width = top_blocks.shape
    columns = top_rhs.shape[2]
    return pl.pallas_call(
        chain_kernel,
        out_shape=[
            jax.ShapeDtypeStruct((tops * size, width), BF16),
            jax.ShapeDtypeStruct((tops * size, columns), F32),
        ],
        scratch_shapes=[pltpu.VMEM((tops * size, columns), BF16)],
        compiler_params=params(),
        cost_estimate=pl.CostEstimate(flops=2 * 10**11, bytes_accessed=10**8, transcendentals=0),
        name="chain_blocks",
    )(top_inverse, top_chain, top_blocks, top_rhs)


def level_one_kernel(count, rhs_ref, inverse_ref, mixed_ref, *refs):
    parts, (out_ref, terms_ref, resid_ref) = refs[: 2 * count], refs[2 * count :]
    half = parts[0].shape[0]
    for side in range(2):
        total = parts[side * count][...].astype(F32)
        for part in parts[side * count + 1 : (side + 1) * count]:
            total += part[...].astype(F32)
        at = slice(side * half, (side + 1) * half)
        resid_ref[at, :] = (rhs_ref[at, :].astype(F32) - total).astype(BF16)
    resid = resid_ref[...]
    solved = mm(inverse_ref[...], resid).astype(BF16)
    out_ref[...] = solved
    terms_ref[...] = mm(mixed_ref[...], solved).astype(BF16)


def level_one(rhs, inverse, mixed, parts):
    size, width = rhs.shape
    return pl.pallas_call(
        lambda *refs: level_one_kernel(len(parts) // 2, *refs),
        out_shape=[
            jax.ShapeDtypeStruct((size, width), BF16),
            jax.ShapeDtypeStruct((mixed.shape[0], width), BF16),
        ],
        scratch_shapes=[pltpu.VMEM((size, width), BF16)],
        compiler_params=params(),
        name="level_one",
    )(rhs, inverse, mixed, *parts)


def share_kernel(at_ref, chained_ref, terms_ref, out_ref):
    total = terms_ref[0].astype(F32)
    for index in range(1, terms_ref.shape[0]):
        total += terms_ref[index].astype(F32)
    out_ref[...] = jnp.broadcast_to((chained_ref[...] - total).astype(BF16)[None], out_ref.shape)


def top_share(member, chained, terms):
    members, chunk, width = terms.shape
    return pl.pallas_call(
        share_kernel,
        grid_spec=pltpu.PrefetchScalarGridSpec(
            num_scalar_prefetch=1,
            grid=(1,),
            in_specs=[
                pl.BlockSpec((chunk, width), lambda i, at: (at[0], 0)),
                pl.BlockSpec((members, chunk, width), lambda i, at: (0, 0, 0)),
            ],
            out_specs=pl.BlockSpec((members, chunk, width), lambda i, at: (0, 0, 0)),
        ),
        out_shape=jax.ShapeDtypeStruct((members, chunk, width), BF16),
        compiler_params=params(),
        name="top_share",
    )(member.reshape(1), chained, terms)


def shards(
    rhs_in,
    rhs_target,
    leaf_inverse,
    level_one_blocks,
    level_one_pattern,
    level_one_rhs,
    level_one_inverse,
    top_blocks,
    top_rhs,
    top_inverse,
    top_chain,
):
    everyone = ("grid", "row", "col")
    device_count = lax.axis_size(everyone)
    rows, cols = lax.axis_size("row"), lax.axis_size("col")
    row, col = lax.axis_index("row"), lax.axis_index("col")
    team = ("grid", "row")

    def along(value, axis, step):
        size = lax.axis_size(axis)
        return lax.ppermute(value, axis, [(i, (i + step) % size) for i in range(size)])

    blocks, pattern = level_one_blocks[0, 0, 0], level_one_pattern[0, 0, 0].T
    far_first, far_second, after, before = pick(row, pattern, blocks)
    rhs_in, far_first, far_second, after, before = lax.optimization_barrier(
        (rhs_in, far_first, far_second, after, before)
    )
    far_first, far_second = along(far_first, "row", 1), along(far_second, "row", -1)
    after, before = along(after, "row", 1), along(before, "row", -1)
    send = route(rhs_target, rhs_in, device_count)
    local_rows, wide = send.shape
    got = lax.all_to_all(
        send.reshape(device_count, local_rows // device_count, wide),
        everyone,
        split_axis=0,
        concat_axis=0,
        tiled=True,
    ).reshape(local_rows, wide)
    top_inverse, far_first, far_second = lax.optimization_barrier((top_inverse, far_first, far_second))
    far_first, far_second = along(far_first, "row", 1), along(far_second, "row", -1)
    mixed, chained_rhs = chain_blocks(top_inverse, top_chain, top_blocks[0, 0], top_rhs)
    got, mixed, chained_rhs = lax.optimization_barrier((got, mixed, chained_rhs))
    leaf_solution = leaf_solve(got, leaf_inverse)

    upper, lower = couple(
        col, row, cols, pattern, leaf_solution, [[blocks], [after], [far_first, far_second], [before]]
    )
    upper = [upper[0]] + [along(upper[step], "col", step) for step in range(1, cols)]
    lower = [lower[0]] + [along(lower[step], "row", -step) for step in range(1, rows)]
    upper, lower = half_sums(upper, lower)
    upper = [upper[0]] + [along(upper[step], "row", -step) for step in range(1, rows)]
    lower = [lower[0]] + [along(lower[step], "col", step) for step in range(1, cols)]
    parts = upper + lower

    solution_one, terms = level_one(level_one_rhs[0, 0], level_one_inverse[0, 0], mixed, parts)
    members = lax.axis_size(team)
    terms = lax.all_to_all(
        terms.reshape(members, terms.shape[0] // members, terms.shape[1]), team, split_axis=0, concat_axis=0, tiled=True
    )
    share = top_share(lax.axis_index(team), chained_rhs, terms)
    top_solution = lax.all_to_all(share, team, split_axis=0, concat_axis=0, tiled=True)
    return (leaf_solution, solution_one[None, None], top_solution.reshape(top_rhs.shape))


def solution(mesh):
    in_specs = (
        P(("grid", "row", "col"), None),
        P(("grid", "row", "col")),
        P(("grid", "row", "col"), None, None),
        P("grid", "row", "col", None, None, None, None),
        P("grid", "row", "col", None, None),
        P("grid", "row", None, "col"),
        P("grid", "row", None, None),
        P("grid", "row", None, None, None),
        P(None, None, "col"),
        P(),
        P(),
    )
    out_specs = (
        P(("grid", "row", "col"), None),
        P("grid", "row", None, "col"),
        P(None, None, "col"),
    )
    return jax.shard_map(shards, mesh=mesh, in_specs=in_specs, out_specs=out_specs, check_vma=False)
```

```python
import jax
import jax.numpy as jnp
from jax import lax
from jax.experimental import pallas as pl
from jax.experimental.pallas import tpu as pltpu
from jax.sharding import PartitionSpec as P

F32 = jnp.float32
BF16 = jnp.bfloat16
LANES = 128
VMEM_LIMIT = 56 * 1024 * 1024
SHORT = pl.CostEstimate(flops=0, bytes_accessed=4 * 10**6, transcendentals=0)
LONG = pl.CostEstimate(flops=2 * 10**11, bytes_accessed=10**8, transcendentals=0)


def params():
    return pltpu.CompilerParams(vmem_limit_bytes=VMEM_LIMIT)


def mm(a, b):
    return jnp.dot(a, b, preferred_element_type=F32)


def mm_nt(a, b):
    return lax.dot_general(a, b, (((1,), (1,)), ((), ())), preferred_element_type=F32)


def pick_kernel(steps, row_ref, pattern_ref, block_ref, *outs):
    rows, leaves, size = pattern_ref.shape[1], block_ref.shape[1], block_ref.shape[2]
    for index, step in enumerate(steps):

        @pl.when(pl.program_id(0) == index)
        def _():
            for leaf in range(leaves):
                present = pattern_ref[leaf, (row_ref[0] + step) % rows].astype(F32).astype(BF16)
                outs[index][:, leaf * size : (leaf + 1) * size] = block_ref[0, leaf] * present


def pick(row, pattern, blocks, steps, cost):
    rows, leaves, size, _ = blocks.shape
    wide = (size, leaves * size)
    stride = steps[-1] - steps[0]
    return pl.pallas_call(
        lambda *refs: pick_kernel(steps, *refs),
        grid_spec=pltpu.PrefetchScalarGridSpec(
            num_scalar_prefetch=2,
            grid=(len(steps),),
            in_specs=[
                pl.BlockSpec(
                    (1, leaves, size, size),
                    lambda i, at, pattern: ((at[0] + steps[0] + stride * i) % rows, 0, 0, 0),
                )
            ],
            out_specs=[pl.BlockSpec(wide, lambda i, at, pattern: (0, 0))] * len(steps),
        ),
        out_shape=[jax.ShapeDtypeStruct(wide, BF16)] * len(steps),
        compiler_params=params(),
        cost_estimate=cost,
        name="pick",
    )(row.reshape(1), pattern, blocks)


def route_kernel(device_count, target_ref, rows_ref, out_ref, slot_ref):
    count = target_ref.shape[1]
    share = count // device_count
    part = out_ref.shape[0]
    width = rows_ref.shape[1]
    step = pl.program_id(0)

    @pl.when(step == 0)
    def _():
        target = target_ref[...]
        owner = target // count
        place = target % count
        piece = 2 * LANES
        before = (
            lax.broadcasted_iota(jnp.int32, (piece, piece), 0)
            < lax.broadcasted_iota(jnp.int32, (piece, piece), 1)
        ).astype(BF16)
        device = lax.broadcasted_iota(jnp.int32, (device_count, piece), 0)
        base = device[:, :1].astype(F32) * share
        for first in range(0, count, piece):
            mine = (device == owner[:, first : first + piece]).astype(F32)
            rank = mm(mine.astype(BF16), before) + base
            slot_ref[0:1, first : first + piece] = jnp.sum(mine * rank, axis=0, keepdims=True)
            base = base + jnp.sum(mine, axis=1, keepdims=True)
        slot_ref[1:2, :] = (place // 32).astype(F32)
        slot_ref[2:3, :] = (place % 32).astype(F32)

    slot = slot_ref[0:1, :].astype(jnp.int32)
    rows_at = lax.broadcasted_iota(jnp.int32, (part, count), 0) + step * part
    pick = (rows_at == slot).astype(BF16)
    out_ref[:, :width] = mm(pick, rows_ref[...]).astype(BF16)
    which = lax.broadcasted_iota(jnp.int32, (LANES, count), 0)
    digits = jnp.where(which == 0, slot_ref[1:2, :], jnp.where(which == 1, slot_ref[2:3, :], 0.0))
    out_ref[:, width:] = mm_nt(pick, digits.astype(BF16)).astype(BF16)


def route(rhs_target, rhs_in, device_count):
    rows, width = rhs_in.shape
    parts = 4
    return pl.pallas_call(
        lambda *refs: route_kernel(device_count, *refs),
        grid=(parts,),
        in_specs=[
            pl.BlockSpec((1, rows), lambda i: (0, 0)),
            pl.BlockSpec((rows, width), lambda i: (0, 0)),
        ],
        out_specs=pl.BlockSpec((rows // parts, width + LANES), lambda i: (i, 0)),
        out_shape=jax.ShapeDtypeStruct((rows, width + LANES), BF16),
        scratch_shapes=[pltpu.VMEM((8, rows), F32)],
        compiler_params=params(),
        name="route",
    )(rhs_target.reshape(1, rows), rhs_in)


def leaf_near_kernel(cols, at_ref, digits_ref, inverse_ref, got_ref, *refs):
    factors, solved_ref, outs, mixed_ref = refs[:3], refs[3], refs[4:-1], refs[-1]
    upper, lower = outs[:cols], outs[cols:]
    leaves, size = inverse_ref.shape[0], inverse_ref.shape[1]
    count, half = leaves * size, size // 2

    @pl.when(pl.program_id(0) == 0)
    def _():
        lane = lax.broadcasted_iota(jnp.int32, (8, LANES), 1)
        weights = jnp.where(lane == 0, 32.0, jnp.where(lane == 1, 1.0, 0.0)).astype(BF16)
        place = mm_nt(weights, digits_ref[...])[0:1, :].astype(jnp.int32)
        for leaf in range(leaves):
            at = slice(leaf * size, (leaf + 1) * size)
            rows_at = lax.broadcasted_iota(jnp.int32, (size, count), 0) + leaf * size
            pick_here = (rows_at == place).astype(BF16)
            mixed_ref[at, :] = mm(inverse_ref[leaf], pick_here).astype(BF16)

    solved_ref[...] = mm(mixed_ref[...], got_ref[...]).astype(BF16)
    for offset in range(cols):

        @pl.when(pl.program_id(0) == offset)
        def _():
            for index, factor in enumerate(factors):
                total = mm(factor[...], solved_ref[...])
                upper[offset][index] = total[:half].astype(BF16)
                lower[index][offset] = total[half:].astype(BF16)


def leaf_near(col, cols, got, leaf_inverse, factors):
    count = got.shape[0]
    width = got.shape[1] - LANES
    block = width // cols
    leaves, size, _ = leaf_inverse.shape
    near = len(factors)
    shapes = [(near, size // 2, block)] * cols + [(cols, size // 2, block)] * near
    outs = pl.pallas_call(
        lambda *refs: leaf_near_kernel(cols, *refs),
        grid_spec=pltpu.PrefetchScalarGridSpec(
            num_scalar_prefetch=1,
            grid=(cols,),
            in_specs=[
                pl.BlockSpec((count, LANES), lambda i, at: (0, width // LANES)),
                pl.BlockSpec((leaves, size, size), lambda i, at: (0, 0, 0)),
                pl.BlockSpec((count, block), lambda i, at: (0, (at[0] + i) % cols)),
            ]
            + [pl.BlockSpec((size, leaves * size), lambda i, at: (0, 0))] * near,
            out_specs=[pl.BlockSpec((count, block), lambda i, at: (0, (at[0] + i) % cols))]
            + [pl.BlockSpec(shape, lambda i, at: (0, 0, 0)) for shape in shapes],
            scratch_shapes=[pltpu.VMEM((count, count), BF16)],
        ),
        out_shape=[jax.ShapeDtypeStruct((count, width), BF16)] + [jax.ShapeDtypeStruct(shape, BF16) for shape in shapes],
        compiler_params=params(),
        name="leaf_near",
    )(col.reshape(1), got, leaf_inverse, got, *factors)
    return outs[0], outs[1 : 1 + cols], outs[1 + cols :]


def couple_far_kernel(cols, at_ref, solved_ref, factor_ref, *outs):
    for offset in range(cols):

        @pl.when(pl.program_id(0) == offset)
        def _():
            outs[offset][0] = mm(factor_ref[...], solved_ref[...]).astype(BF16)


def couple_far(col, cols, solved, factor):
    count, width = solved.shape
    block = width // cols
    shape = (1, factor.shape[0], block)
    return pl.pallas_call(
        lambda *refs: couple_far_kernel(cols, *refs),
        grid_spec=pltpu.PrefetchScalarGridSpec(
            num_scalar_prefetch=1,
            grid=(cols,),
            in_specs=[
                pl.BlockSpec((count, block), lambda i, at: (0, (at[0] + i) % cols)),
                pl.BlockSpec(factor.shape, lambda i, at: (0, 0)),
            ],
            out_specs=[pl.BlockSpec(shape, lambda i, at: (0, 0, 0))] * cols,
        ),
        out_shape=[jax.ShapeDtypeStruct(shape, BF16)] * cols,
        compiler_params=params(),
        name="couple_far",
    )(col.reshape(1), solved, factor)


def part_sums_kernel(count, *refs):
    parts, outs = refs[:count], refs[count:]
    for index, out in enumerate(outs):
        total = parts[0][index].astype(F32)
        for part in parts[1:]:
            total += part[index].astype(F32)
        out[...] = total.astype(out.dtype)


def part_sums(parts, kept):
    shape = parts[0].shape[1:]
    return pl.pallas_call(
        lambda *refs: part_sums_kernel(len(parts), *refs),
        out_shape=[
            jax.ShapeDtypeStruct(shape, F32 if index == 0 and kept else BF16) for index in range(parts[0].shape[0])
        ],
        compiler_params=params(),
        name="part_sums",
    )(*parts)


def chain_kernel(inverse_ref, chain_ref, blocks_ref, rhs_ref, mixed_ref, chained_ref, solved_ref):
    tops, size = inverse_ref.shape[0], inverse_ref.shape[1]
    for now in range(tops):
        left = blocks_ref[now].astype(F32)
        right = rhs_ref[now].astype(F32)
        for earlier in range(now):
            link = chain_ref[now * (now - 1) // 2 + earlier]
            at = slice(earlier * size, (earlier + 1) * size)
            left = left - mm(link, mixed_ref[at, :])
            right = right - mm(link, solved_ref[at, :])
        inverse = inverse_ref[now]
        at = slice(now * size, (now + 1) * size)
        mixed_ref[at, :] = mm(inverse, left.astype(BF16)).astype(BF16)
        answer = mm(inverse, right.astype(BF16))
        solved_ref[at, :] = answer.astype(BF16)
        chained_ref[at, :] = answer


def chain_blocks(top_inverse, top_chain, top_blocks, top_rhs):
    tops, size, width = top_blocks.shape
    columns = top_rhs.shape[2]
    return pl.pallas_call(
        chain_kernel,
        out_shape=[
            jax.ShapeDtypeStruct((tops * size, width), BF16),
            jax.ShapeDtypeStruct((tops * size, columns), F32),
        ],
        scratch_shapes=[pltpu.VMEM((tops * size, columns), BF16)],
        compiler_params=params(),
        name="chain_blocks",
    )(top_inverse, top_chain, top_blocks, top_rhs)


def level_one_kernel(counts, rhs_ref, inverse_ref, mixed_ref, far_ref, *refs):
    parts, (out_ref, terms_ref, resid_ref) = refs[: sum(counts)], refs[sum(counts) :]
    half = parts[0].shape[0]
    first = 0
    for side, count in enumerate(counts):
        at = slice(side * half, (side + 1) * half)
        total = far_ref[at, :].astype(F32)
        for part in parts[first : first + count]:
            total += part[...].astype(F32)
        resid_ref[at, :] = (rhs_ref[at, :].astype(F32) - total).astype(BF16)
        first += count
    solved = mm(inverse_ref[...], resid_ref[...]).astype(BF16)
    out_ref[...] = solved
    terms_ref[...] = mm(mixed_ref[...], solved).astype(BF16)


def level_one(rhs, inverse, mixed, far, upper, lower):
    size, width = rhs.shape
    counts = (len(upper), len(lower))
    return pl.pallas_call(
        lambda *refs: level_one_kernel(counts, *refs),
        out_shape=[
            jax.ShapeDtypeStruct((size, width), BF16),
            jax.ShapeDtypeStruct((mixed.shape[0], width), BF16),
        ],
        scratch_shapes=[pltpu.VMEM((size, width), BF16)],
        compiler_params=params(),
        name="level_one",
    )(rhs, inverse, mixed, far, *upper, *lower)


def share_kernel(at_ref, chained_ref, terms_ref, out_ref):
    total = terms_ref[0].astype(F32)
    for index in range(1, terms_ref.shape[0]):
        total += terms_ref[index].astype(F32)
    out_ref[...] = jnp.broadcast_to((chained_ref[...] - total).astype(BF16)[None], out_ref.shape)


def top_share(member, chained, terms):
    members, chunk, width = terms.shape
    return pl.pallas_call(
        share_kernel,
        grid_spec=pltpu.PrefetchScalarGridSpec(
            num_scalar_prefetch=1,
            grid=(1,),
            in_specs=[
                pl.BlockSpec((chunk, width), lambda i, at: (at[0], 0)),
                pl.BlockSpec((members, chunk, width), lambda i, at: (0, 0, 0)),
            ],
            out_specs=pl.BlockSpec((members, chunk, width), lambda i, at: (0, 0, 0)),
        ),
        out_shape=jax.ShapeDtypeStruct((members, chunk, width), BF16),
        compiler_params=params(),
        name="top_share",
    )(member.reshape(1), chained, terms)


def shards(
    rhs_in,
    rhs_target,
    leaf_inverse,
    level_one_blocks,
    level_one_pattern,
    level_one_rhs,
    level_one_inverse,
    top_blocks,
    top_rhs,
    top_inverse,
    top_chain,
):
    everyone = ("grid", "row", "col")
    device_count = lax.axis_size(everyone)
    rows, cols = lax.axis_size("row"), lax.axis_size("col")
    row, col = lax.axis_index("row"), lax.axis_index("col")
    team = ("grid", "row")

    def along(value, axis, step):
        size = lax.axis_size(axis)
        return lax.ppermute(value, axis, [(i, (i + step) % size) for i in range(size)])

    blocks, pattern = level_one_blocks[0, 0, 0], level_one_pattern[0, 0, 0].T
    after, before = pick(row, pattern, blocks, (1, rows - 1), SHORT)
    rhs_in, after, before = lax.optimization_barrier((rhs_in, after, before))
    after, before = along(after, "row", 1), along(before, "row", -1)
    send = route(rhs_target, rhs_in, device_count)
    local_rows, wide = send.shape
    got = lax.all_to_all(
        send.reshape(device_count, local_rows // device_count, wide),
        everyone,
        split_axis=0,
        concat_axis=0,
        tiled=True,
    ).reshape(local_rows, wide)
    mixed, chained_rhs = chain_blocks(top_inverse, top_chain, top_blocks[0, 0], top_rhs)
    after, before, blocks, mixed, chained_rhs = lax.optimization_barrier((after, before, blocks, mixed, chained_rhs))
    own, far = pick(row, pattern, blocks, (0, rows // 2), LONG)
    got, own, far = lax.optimization_barrier((got, own, far))
    far = along(far, "row", rows // 2)

    def over_cols(parts):
        return [parts[0]] + [along(part, "col", step) for step, part in enumerate(parts[1:], 1)]

    leaf_solution, upper, lower = leaf_near(col, cols, got, leaf_inverse, (own, after, before))
    upper = over_cols(upper)
    lower = [lower[0], along(lower[1], "row", -1), along(lower[2], "row", 1)]
    opposite = over_cols(couple_far(col, cols, leaf_solution, far))
    mine, to_last, to_next = part_sums(upper, True)
    lower = part_sums(lower, True)
    opposite, _ = lax.optimization_barrier((opposite, lower[0]))
    upper = [mine, along(to_last, "row", -1), along(to_next, "row", 1)]
    lower = over_cols(lower)
    (to_far,) = part_sums(opposite, False)
    opposite = along(to_far, "row", rows // 2)

    solution_one, terms = level_one(level_one_rhs[0, 0], level_one_inverse[0, 0], mixed, opposite, upper, lower)
    members = lax.axis_size(team)
    terms = lax.all_to_all(
        terms.reshape(members, terms.shape[0] // members, terms.shape[1]), team, split_axis=0, concat_axis=0, tiled=True
    )
    share = top_share(lax.axis_index(team), chained_rhs, terms)
    top_solution = lax.all_to_all(share, team, split_axis=0, concat_axis=0, tiled=True)
    return (leaf_solution, solution_one[None, None], top_solution.reshape(top_rhs.shape))


def solution(mesh):
    in_specs = (
        P(("grid", "row", "col"), None),
        P(("grid", "row", "col")),
        P(("grid", "row", "col"), None, None),
        P("grid", "row", "col", None, None, None, None),
        P("grid", "row", "col", None, None),
        P("grid", "row", None, "col"),
        P("grid", "row", None, None),
        P("grid", "row", None, None, None),
        P(None, None, "col"),
        P(),
        P(),
    )
    out_specs = (
        P(("grid", "row", "col"), None),
        P("grid", "row", None, "col"),
        P(None, None, "col"),
    )
    return jax.shard_map(shards, mesh=mesh, in_specs=in_specs, out_specs=out_specs, check_vma=False)
```

```python
import jax
import jax.numpy as jnp
from jax import lax
from jax.experimental import pallas as pl
from jax.experimental.pallas import tpu as pltpu
from jax.sharding import PartitionSpec as P

F32 = jnp.float32
BF16 = jnp.bfloat16
LANES = 128
VMEM_LIMIT = 56 * 1024 * 1024
SHORT = pl.CostEstimate(flops=0, bytes_accessed=4 * 10**6, transcendentals=0)
LONG = pl.CostEstimate(flops=2 * 10**11, bytes_accessed=10**8, transcendentals=0)


def params():
    return pltpu.CompilerParams(vmem_limit_bytes=VMEM_LIMIT)


def mm(a, b):
    return jnp.dot(a, b, preferred_element_type=F32)


def mm_nt(a, b):
    return lax.dot_general(a, b, (((1,), (1,)), ((), ())), preferred_element_type=F32)


def pick_kernel(steps, row_ref, pattern_ref, block_ref, *outs):
    rows, leaves, size = pattern_ref.shape[1], block_ref.shape[1], block_ref.shape[2]
    for index, step in enumerate(steps):

        @pl.when(pl.program_id(0) == index)
        def _():
            for leaf in range(leaves):
                present = pattern_ref[leaf, (row_ref[0] + step) % rows].astype(F32).astype(BF16)
                outs[index][:, leaf * size : (leaf + 1) * size] = block_ref[0, leaf] * present


def pick(row, pattern, blocks, steps, cost):
    rows, leaves, size, _ = blocks.shape
    wide = (size, leaves * size)
    stride = steps[-1] - steps[0]
    return pl.pallas_call(
        lambda *refs: pick_kernel(steps, *refs),
        grid_spec=pltpu.PrefetchScalarGridSpec(
            num_scalar_prefetch=2,
            grid=(len(steps),),
            in_specs=[
                pl.BlockSpec(
                    (1, leaves, size, size),
                    lambda i, at, pattern: ((at[0] + steps[0] + stride * i) % rows, 0, 0, 0),
                )
            ],
            out_specs=[pl.BlockSpec(wide, lambda i, at, pattern: (0, 0))] * len(steps),
        ),
        out_shape=[jax.ShapeDtypeStruct(wide, BF16)] * len(steps),
        compiler_params=params(),
        cost_estimate=cost,
        name="pick",
    )(row.reshape(1), pattern, blocks)


def route_kernel(device_count, target_ref, rows_ref, out_ref, slot_ref):
    count = target_ref.shape[1]
    share = count // device_count
    part = out_ref.shape[0]
    width = rows_ref.shape[1]
    step = pl.program_id(0)

    @pl.when(step == 0)
    def _():
        target = target_ref[...]
        owner = target // count
        place = target % count
        piece = 2 * LANES
        before = (
            lax.broadcasted_iota(jnp.int32, (piece, piece), 0)
            < lax.broadcasted_iota(jnp.int32, (piece, piece), 1)
        ).astype(BF16)
        device = lax.broadcasted_iota(jnp.int32, (device_count, piece), 0)
        base = device[:, :1].astype(F32) * share
        for first in range(0, count, piece):
            mine = (device == owner[:, first : first + piece]).astype(F32)
            rank = mm(mine.astype(BF16), before) + base
            slot_ref[0:1, first : first + piece] = jnp.sum(mine * rank, axis=0, keepdims=True)
            base = base + jnp.sum(mine, axis=1, keepdims=True)
        slot_ref[1:2, :] = (place // 32).astype(F32)
        slot_ref[2:3, :] = (place % 32).astype(F32)

    slot = slot_ref[0:1, :].astype(jnp.int32)
    rows_at = lax.broadcasted_iota(jnp.int32, (part, count), 0) + step * part
    pick = (rows_at == slot).astype(BF16)
    out_ref[:, :width] = mm(pick, rows_ref[...]).astype(BF16)
    which = lax.broadcasted_iota(jnp.int32, (LANES, count), 0)
    digits = jnp.where(which == 0, slot_ref[1:2, :], jnp.where(which == 1, slot_ref[2:3, :], 0.0))
    out_ref[:, width:] = mm_nt(pick, digits.astype(BF16)).astype(BF16)


def route(rhs_target, rhs_in, device_count):
    rows, width = rhs_in.shape
    parts = 4
    return pl.pallas_call(
        lambda *refs: route_kernel(device_count, *refs),
        grid=(parts,),
        in_specs=[
            pl.BlockSpec((1, rows), lambda i: (0, 0)),
            pl.BlockSpec((rows, width), lambda i: (0, 0)),
        ],
        out_specs=pl.BlockSpec((rows // parts, width + LANES), lambda i: (i, 0)),
        out_shape=jax.ShapeDtypeStruct((rows, width + LANES), BF16),
        scratch_shapes=[pltpu.VMEM((8, rows), F32)],
        compiler_params=params(),
        name="route",
    )(rhs_target.reshape(1, rows), rhs_in)


def leaf_near_kernel(cols, at_ref, digits_ref, inverse_ref, got_ref, *refs):
    factors, solved_ref, outs, mixed_ref = refs[:3], refs[3], refs[4:-1], refs[-1]
    upper, lower = outs[:cols], outs[cols:]
    leaves, size = inverse_ref.shape[0], inverse_ref.shape[1]
    count, half = leaves * size, size // 2

    @pl.when(pl.program_id(0) == 0)
    def _():
        lane = lax.broadcasted_iota(jnp.int32, (8, LANES), 1)
        weights = jnp.where(lane == 0, 32.0, jnp.where(lane == 1, 1.0, 0.0)).astype(BF16)
        place = mm_nt(weights, digits_ref[...])[0:1, :].astype(jnp.int32)
        for leaf in range(leaves):
            at = slice(leaf * size, (leaf + 1) * size)
            rows_at = lax.broadcasted_iota(jnp.int32, (size, count), 0) + leaf * size
            pick_here = (rows_at == place).astype(BF16)
            mixed_ref[at, :] = mm(inverse_ref[leaf], pick_here).astype(BF16)

    solved_ref[...] = mm(mixed_ref[...], got_ref[...]).astype(BF16)
    for offset in range(cols):

        @pl.when(pl.program_id(0) == offset)
        def _():
            for index, factor in enumerate(factors):
                total = mm(factor[...], solved_ref[...])
                upper[offset][index] = total[:half].astype(BF16)
                lower[index][(at_ref[0] + offset) % cols] = total[half:].astype(BF16)


def leaf_near(col, cols, got, leaf_inverse, factors):
    count = got.shape[0]
    width = got.shape[1] - LANES
    block = width // cols
    leaves, size, _ = leaf_inverse.shape
    near = len(factors)
    shapes = [(near, size // 2, block)] * cols + [(cols, size // 2, block)] * near
    outs = pl.pallas_call(
        lambda *refs: leaf_near_kernel(cols, *refs),
        grid_spec=pltpu.PrefetchScalarGridSpec(
            num_scalar_prefetch=1,
            grid=(cols,),
            in_specs=[
                pl.BlockSpec((count, LANES), lambda i, at: (0, width // LANES)),
                pl.BlockSpec((leaves, size, size), lambda i, at: (0, 0, 0)),
                pl.BlockSpec((count, block), lambda i, at: (0, (at[0] + i) % cols)),
            ]
            + [pl.BlockSpec((size, leaves * size), lambda i, at: (0, 0))] * near,
            out_specs=[pl.BlockSpec((count, block), lambda i, at: (0, (at[0] + i) % cols))]
            + [pl.BlockSpec(shape, lambda i, at: (0, 0, 0)) for shape in shapes],
            scratch_shapes=[pltpu.VMEM((count, count), BF16)],
        ),
        out_shape=[jax.ShapeDtypeStruct((count, width), BF16)] + [jax.ShapeDtypeStruct(shape, BF16) for shape in shapes],
        compiler_params=params(),
        name="leaf_near",
    )(col.reshape(1), got, leaf_inverse, got, *factors)
    return outs[0], outs[1 : 1 + cols], outs[1 + cols :]


def couple_far_kernel(cols, at_ref, solved_ref, factor_ref, *outs):
    for offset in range(cols):

        @pl.when(pl.program_id(0) == offset)
        def _():
            outs[offset][0] = mm(factor_ref[...], solved_ref[...]).astype(BF16)


def couple_far(col, cols, solved, factor):
    count, width = solved.shape
    block = width // cols
    shape = (1, factor.shape[0], block)
    return pl.pallas_call(
        lambda *refs: couple_far_kernel(cols, *refs),
        grid_spec=pltpu.PrefetchScalarGridSpec(
            num_scalar_prefetch=1,
            grid=(cols,),
            in_specs=[
                pl.BlockSpec((count, block), lambda i, at: (0, (at[0] + i) % cols)),
                pl.BlockSpec(factor.shape, lambda i, at: (0, 0)),
            ],
            out_specs=[pl.BlockSpec(shape, lambda i, at: (0, 0, 0))] * cols,
        ),
        out_shape=[jax.ShapeDtypeStruct(shape, BF16)] * cols,
        compiler_params=params(),
        cost_estimate=LONG,
        name="couple_far",
    )(col.reshape(1), solved, factor)


def part_sums_kernel(count, *refs):
    parts, outs = refs[:count], refs[count:]
    for index in range(parts[0].shape[0]):
        total = parts[0][index].astype(F32)
        for part in parts[1:]:
            total += part[index].astype(F32)
        if len(outs) == 1:
            outs[0][index] = total.astype(BF16)
        else:
            outs[index][...] = total.astype(outs[index].dtype)


def part_sums(parts, apart, cost=None):
    count, rows, width = parts[0].shape
    shapes = [((rows, width), F32 if index == 0 else BF16) for index in range(count)]
    if not apart:
        shapes = [((count, rows, width), BF16)]
    return pl.pallas_call(
        lambda *refs: part_sums_kernel(len(parts), *refs),
        out_shape=[jax.ShapeDtypeStruct(*shape) for shape in shapes],
        compiler_params=params(),
        cost_estimate=cost,
        name="part_sums",
    )(*parts)


def chain_kernel(inverse_ref, chain_ref, blocks_ref, rhs_ref, mixed_ref, chained_ref, solved_ref):
    tops, size = inverse_ref.shape[0], inverse_ref.shape[1]
    for now in range(tops):
        left = blocks_ref[now].astype(F32)
        right = rhs_ref[now].astype(F32)
        for earlier in range(now):
            link = chain_ref[now * (now - 1) // 2 + earlier]
            at = slice(earlier * size, (earlier + 1) * size)
            left = left - mm(link, mixed_ref[at, :])
            right = right - mm(link, solved_ref[at, :])
        inverse = inverse_ref[now]
        at = slice(now * size, (now + 1) * size)
        mixed_ref[at, :] = mm(inverse, left.astype(BF16)).astype(BF16)
        answer = mm(inverse, right.astype(BF16))
        solved_ref[at, :] = answer.astype(BF16)
        chained_ref[at, :] = answer


def chain_blocks(top_inverse, top_chain, top_blocks, top_rhs):
    tops, size, width = top_blocks.shape
    columns = top_rhs.shape[2]
    return pl.pallas_call(
        chain_kernel,
        out_shape=[
            jax.ShapeDtypeStruct((tops * size, width), BF16),
            jax.ShapeDtypeStruct((tops * size, columns), F32),
        ],
        scratch_shapes=[pltpu.VMEM((tops * size, columns), BF16)],
        compiler_params=params(),
        name="chain_blocks",
    )(top_inverse, top_chain, top_blocks, top_rhs)


def level_one_kernel(count, rhs_ref, inverse_ref, mixed_ref, far_ref, lower_ref, *refs):
    upper, (out_ref, terms_ref, resid_ref) = refs[:count], refs[count:]
    half = lower_ref.shape[1]
    lower = [lower_ref.at[index] for index in range(lower_ref.shape[0])]
    for side, parts in enumerate((upper, lower)):
        at = slice(side * half, (side + 1) * half)
        total = far_ref[0, at, :].astype(F32)
        for part in parts:
            total += part[...].astype(F32)
        resid_ref[at, :] = (rhs_ref[at, :].astype(F32) - total).astype(BF16)
    solved = mm(inverse_ref[...], resid_ref[...]).astype(BF16)
    out_ref[...] = solved
    terms_ref[...] = mm(mixed_ref[...], solved).astype(BF16)


def level_one(rhs, inverse, mixed, far, upper, lower):
    size, width = rhs.shape
    return pl.pallas_call(
        lambda *refs: level_one_kernel(len(upper), *refs),
        out_shape=[
            jax.ShapeDtypeStruct((size, width), BF16),
            jax.ShapeDtypeStruct((mixed.shape[0], width), BF16),
        ],
        scratch_shapes=[pltpu.VMEM((size, width), BF16)],
        compiler_params=params(),
        name="level_one",
    )(rhs, inverse, mixed, far, lower, *upper)


def share_kernel(at_ref, chained_ref, terms_ref, out_ref):
    total = terms_ref[0].astype(F32)
    for index in range(1, terms_ref.shape[0]):
        total += terms_ref[index].astype(F32)
    out_ref[...] = jnp.broadcast_to((chained_ref[...] - total).astype(BF16)[None], out_ref.shape)


def top_share(member, chained, terms):
    members, chunk, width = terms.shape
    return pl.pallas_call(
        share_kernel,
        grid_spec=pltpu.PrefetchScalarGridSpec(
            num_scalar_prefetch=1,
            grid=(1,),
            in_specs=[
                pl.BlockSpec((chunk, width), lambda i, at: (at[0], 0)),
                pl.BlockSpec((members, chunk, width), lambda i, at: (0, 0, 0)),
            ],
            out_specs=pl.BlockSpec((members, chunk, width), lambda i, at: (0, 0, 0)),
        ),
        out_shape=jax.ShapeDtypeStruct((members, chunk, width), BF16),
        compiler_params=params(),
        name="top_share",
    )(member.reshape(1), chained, terms)


def shards(
    rhs_in,
    rhs_target,
    leaf_inverse,
    level_one_blocks,
    level_one_pattern,
    level_one_rhs,
    level_one_inverse,
    top_blocks,
    top_rhs,
    top_inverse,
    top_chain,
):
    everyone = ("grid", "row", "col")
    device_count = lax.axis_size(everyone)
    rows, cols = lax.axis_size("row"), lax.axis_size("col")
    row, col = lax.axis_index("row"), lax.axis_index("col")
    team = ("grid", "row")

    def along(value, axis, step):
        size = lax.axis_size(axis)
        return lax.ppermute(value, axis, [(i, (i + step) % size) for i in range(size)])

    blocks, pattern = level_one_blocks[0, 0, 0], level_one_pattern[0, 0, 0].T
    after, before = pick(row, pattern, blocks, (1, rows - 1), SHORT)
    rhs_in, after, before = lax.optimization_barrier((rhs_in, after, before))
    after, before = along(after, "row", 1), along(before, "row", -1)
    send = route(rhs_target, rhs_in, device_count)
    local_rows, wide = send.shape
    got = lax.all_to_all(
        send.reshape(device_count, local_rows // device_count, wide),
        everyone,
        split_axis=0,
        concat_axis=0,
        tiled=True,
    ).reshape(local_rows, wide)
    mixed, chained_rhs = chain_blocks(top_inverse, top_chain, top_blocks[0, 0], top_rhs)
    after, before, blocks, mixed, chained_rhs = lax.optimization_barrier((after, before, blocks, mixed, chained_rhs))
    own, far = pick(row, pattern, blocks, (0, rows // 2), LONG)
    got, own, far = lax.optimization_barrier((got, own, far))
    far = along(far, "row", rows // 2)

    def over_cols(parts):
        return [parts[0]] + [along(part, "col", step) for step, part in enumerate(parts[1:], 1)]

    leaf_solution, upper, lower = leaf_near(col, cols, got, leaf_inverse, (own, after, before))
    upper = over_cols(upper)
    later, _ = lax.optimization_barrier((lower[2], far))
    lower = [lower[0], along(lower[1], "row", -1), along(later, "row", 1)]
    opposite = over_cols(couple_far(col, cols, leaf_solution, far))
    mine, to_last, to_next = part_sums(upper, True)
    (lower,) = part_sums(lower, False)
    upper = [mine, along(to_last, "row", -1), along(to_next, "row", 1)]
    opposite, _ = lax.optimization_barrier((opposite, (lower, upper[1], upper[2])))
    lower = lax.all_to_all(lower, "col", split_axis=0, concat_axis=0, tiled=True)
    (to_far,) = part_sums(opposite, False, LONG)
    opposite = along(to_far, "row", rows // 2)

    solution_one, terms = level_one(level_one_rhs[0, 0], level_one_inverse[0, 0], mixed, opposite, upper, lower)
    members = lax.axis_size(team)
    terms = lax.all_to_all(
        terms.reshape(members, terms.shape[0] // members, terms.shape[1]), team, split_axis=0, concat_axis=0, tiled=True
    )
    share = top_share(lax.axis_index(team), chained_rhs, terms)
    top_solution = lax.all_to_all(share, team, split_axis=0, concat_axis=0, tiled=True)
    return (leaf_solution, solution_one[None, None], top_solution.reshape(top_rhs.shape))


def solution(mesh):
    in_specs = (
        P(("grid", "row", "col"), None),
        P(("grid", "row", "col")),
        P(("grid", "row", "col"), None, None),
        P("grid", "row", "col", None, None, None, None),
        P("grid", "row", "col", None, None),
        P("grid", "row", None, "col"),
        P("grid", "row", None, None),
        P("grid", "row", None, None, None),
        P(None, None, "col"),
        P(),
        P(),
    )
    out_specs = (
        P(("grid", "row", "col"), None),
        P("grid", "row", None, "col"),
        P(None, None, "col"),
    )
    return jax.shard_map(shards, mesh=mesh, in_specs=in_specs, out_specs=out_specs, check_vma=False)
```

```python
import jax
import jax.numpy as jnp
from jax import lax
from jax.experimental import pallas as pl
from jax.experimental.pallas import tpu as pltpu
from jax.sharding import PartitionSpec as P

F32 = jnp.float32
BF16 = jnp.bfloat16
LANES = 128
VMEM_LIMIT = 56 * 1024 * 1024
SHORT = pl.CostEstimate(flops=0, bytes_accessed=4 * 10**6, transcendentals=0)
LONG = pl.CostEstimate(flops=2 * 10**11, bytes_accessed=10**8, transcendentals=0)


def params():
    return pltpu.CompilerParams(vmem_limit_bytes=VMEM_LIMIT)


def mm(a, b):
    return jnp.dot(a, b, preferred_element_type=F32)


def mm_nt(a, b):
    return lax.dot_general(a, b, (((1,), (1,)), ((), ())), preferred_element_type=F32)


def pick_kernel(steps, row_ref, pattern_ref, block_ref, *outs):
    rows, leaves, size = pattern_ref.shape[1], block_ref.shape[1], block_ref.shape[2]
    for index, step in enumerate(steps):

        @pl.when(pl.program_id(0) == index)
        def _():
            for leaf in range(leaves):
                present = pattern_ref[leaf, (row_ref[0] + step) % rows].astype(F32).astype(BF16)
                outs[index][:, leaf * size : (leaf + 1) * size] = block_ref[0, leaf] * present


def pick(row, pattern, blocks, steps, cost):
    rows, leaves, size, _ = blocks.shape
    wide = (size, leaves * size)
    stride = steps[-1] - steps[0]
    return pl.pallas_call(
        lambda *refs: pick_kernel(steps, *refs),
        grid_spec=pltpu.PrefetchScalarGridSpec(
            num_scalar_prefetch=2,
            grid=(len(steps),),
            in_specs=[
                pl.BlockSpec(
                    (1, leaves, size, size),
                    lambda i, at, pattern: ((at[0] + steps[0] + stride * i) % rows, 0, 0, 0),
                )
            ],
            out_specs=[pl.BlockSpec(wide, lambda i, at, pattern: (0, 0))] * len(steps),
        ),
        out_shape=[jax.ShapeDtypeStruct(wide, BF16)] * len(steps),
        compiler_params=params(),
        cost_estimate=cost,
        name="pick",
    )(row.reshape(1), pattern, blocks)


def route_kernel(device_count, target_ref, rows_ref, out_ref, slot_ref):
    count = target_ref.shape[1]
    share = count // device_count
    part = out_ref.shape[0]
    width = rows_ref.shape[1]
    step = pl.program_id(0)

    @pl.when(step == 0)
    def _():
        target = target_ref[...]
        owner = target // count
        place = target % count
        piece = 2 * LANES
        before = (
            lax.broadcasted_iota(jnp.int32, (piece, piece), 0)
            < lax.broadcasted_iota(jnp.int32, (piece, piece), 1)
        ).astype(BF16)
        device = lax.broadcasted_iota(jnp.int32, (device_count, piece), 0)
        base = device[:, :1].astype(F32) * share
        for first in range(0, count, piece):
            mine = (device == owner[:, first : first + piece]).astype(F32)
            rank = mm(mine.astype(BF16), before) + base
            slot_ref[0:1, first : first + piece] = jnp.sum(mine * rank, axis=0, keepdims=True)
            base = base + jnp.sum(mine, axis=1, keepdims=True)
        slot_ref[1:2, :] = (place // 32).astype(F32)
        slot_ref[2:3, :] = (place % 32).astype(F32)

    slot = slot_ref[0:1, :].astype(jnp.int32)
    rows_at = lax.broadcasted_iota(jnp.int32, (part, count), 0) + step * part
    pick = (rows_at == slot).astype(BF16)
    out_ref[:, :width] = mm(pick, rows_ref[...]).astype(BF16)
    which = lax.broadcasted_iota(jnp.int32, (LANES, count), 0)
    digits = jnp.where(which == 0, slot_ref[1:2, :], jnp.where(which == 1, slot_ref[2:3, :], 0.0))
    out_ref[:, width:] = mm_nt(pick, digits.astype(BF16)).astype(BF16)


def route(rhs_target, rhs_in, device_count):
    rows, width = rhs_in.shape
    parts = 4
    return pl.pallas_call(
        lambda *refs: route_kernel(device_count, *refs),
        grid=(parts,),
        in_specs=[
            pl.BlockSpec((1, rows), lambda i: (0, 0)),
            pl.BlockSpec((rows, width), lambda i: (0, 0)),
        ],
        out_specs=pl.BlockSpec((rows // parts, width + LANES), lambda i: (i, 0)),
        out_shape=jax.ShapeDtypeStruct((rows, width + LANES), BF16),
        scratch_shapes=[pltpu.VMEM((8, rows), F32)],
        compiler_params=params(),
        name="route",
    )(rhs_target.reshape(1, rows), rhs_in)


def leaf_near_kernel(cols, at_ref, digits_ref, inverse_ref, got_ref, *refs):
    factors, solved_ref, outs, mixed_ref = refs[:3], refs[3], refs[4:-1], refs[-1]
    upper, lower = outs[:cols], outs[cols:]
    leaves, size = inverse_ref.shape[0], inverse_ref.shape[1]
    count, half = leaves * size, size // 2

    @pl.when(pl.program_id(0) == 0)
    def _():
        lane = lax.broadcasted_iota(jnp.int32, (8, LANES), 1)
        weights = jnp.where(lane == 0, 32.0, jnp.where(lane == 1, 1.0, 0.0)).astype(BF16)
        place = mm_nt(weights, digits_ref[...])[0:1, :].astype(jnp.int32)
        for leaf in range(leaves):
            at = slice(leaf * size, (leaf + 1) * size)
            rows_at = lax.broadcasted_iota(jnp.int32, (size, count), 0) + leaf * size
            pick_here = (rows_at == place).astype(BF16)
            mixed_ref[at, :] = mm(inverse_ref[leaf], pick_here).astype(BF16)

    solved_ref[...] = mm(mixed_ref[...], got_ref[...]).astype(BF16)
    for offset in range(cols):

        @pl.when(pl.program_id(0) == offset)
        def _():
            for index, factor in enumerate(factors):
                total = mm(factor[...], solved_ref[...])
                upper[offset][index] = total[:half].astype(BF16)
                lower[index][offset] = total[half:].astype(BF16)


def leaf_near(col, cols, got, leaf_inverse, factors):
    count = got.shape[0]
    width = got.shape[1] - LANES
    block = width // cols
    leaves, size, _ = leaf_inverse.shape
    near = len(factors)
    shapes = [(near, size // 2, block)] * cols + [(cols, size // 2, block)] * near
    outs = pl.pallas_call(
        lambda *refs: leaf_near_kernel(cols, *refs),
        grid_spec=pltpu.PrefetchScalarGridSpec(
            num_scalar_prefetch=1,
            grid=(cols,),
            in_specs=[
                pl.BlockSpec((count, LANES), lambda i, at: (0, width // LANES)),
                pl.BlockSpec((leaves, size, size), lambda i, at: (0, 0, 0)),
                pl.BlockSpec((count, block), lambda i, at: (0, (at[0] + i) % cols)),
            ]
            + [pl.BlockSpec((size, leaves * size), lambda i, at: (0, 0))] * near,
            out_specs=[pl.BlockSpec((count, block), lambda i, at: (0, (at[0] + i) % cols))]
            + [pl.BlockSpec(shape, lambda i, at: (0, 0, 0)) for shape in shapes],
            scratch_shapes=[pltpu.VMEM((count, count), BF16)],
        ),
        out_shape=[jax.ShapeDtypeStruct((count, width), BF16)] + [jax.ShapeDtypeStruct(shape, BF16) for shape in shapes],
        compiler_params=params(),
        name="leaf_near",
    )(col.reshape(1), got, leaf_inverse, got, *factors)
    return outs[0], outs[1 : 1 + cols], outs[1 + cols :]


def couple_far_kernel(cols, at_ref, solved_ref, factor_ref, *outs):
    for offset in range(cols):

        @pl.when(pl.program_id(0) == offset)
        def _():
            outs[offset][0] = mm(factor_ref[...], solved_ref[...]).astype(BF16)


def couple_far(col, cols, solved, factor):
    count, width = solved.shape
    block = width // cols
    shape = (1, factor.shape[0], block)
    return pl.pallas_call(
        lambda *refs: couple_far_kernel(cols, *refs),
        grid_spec=pltpu.PrefetchScalarGridSpec(
            num_scalar_prefetch=1,
            grid=(cols,),
            in_specs=[
                pl.BlockSpec((count, block), lambda i, at: (0, (at[0] + i) % cols)),
                pl.BlockSpec(factor.shape, lambda i, at: (0, 0)),
            ],
            out_specs=[pl.BlockSpec(shape, lambda i, at: (0, 0, 0))] * cols,
        ),
        out_shape=[jax.ShapeDtypeStruct(shape, BF16)] * cols,
        compiler_params=params(),
        cost_estimate=LONG,
        name="couple_far",
    )(col.reshape(1), solved, factor)


def part_sums_kernel(count, *refs):
    parts, outs = refs[:count], refs[count:]
    for index, out in enumerate(outs):
        total = parts[0][index].astype(F32)
        for part in parts[1:]:
            total += part[index].astype(F32)
        out[...] = total.astype(out.dtype)


def part_sums(parts, kept, cost=None):
    shape = parts[0].shape[1:]
    return pl.pallas_call(
        lambda *refs: part_sums_kernel(len(parts), *refs),
        out_shape=[
            jax.ShapeDtypeStruct(shape, F32 if index == 0 and kept else BF16) for index in range(parts[0].shape[0])
        ],
        compiler_params=params(),
        cost_estimate=cost,
        name="part_sums",
    )(*parts)


def chain_kernel(inverse_ref, chain_ref, blocks_ref, rhs_ref, mixed_ref, chained_ref, solved_ref):
    tops, size = inverse_ref.shape[0], inverse_ref.shape[1]
    for now in range(tops):
        left = blocks_ref[now].astype(F32)
        right = rhs_ref[now].astype(F32)
        for earlier in range(now):
            link = chain_ref[now * (now - 1) // 2 + earlier]
            at = slice(earlier * size, (earlier + 1) * size)
            left = left - mm(link, mixed_ref[at, :])
            right = right - mm(link, solved_ref[at, :])
        inverse = inverse_ref[now]
        at = slice(now * size, (now + 1) * size)
        mixed_ref[at, :] = mm(inverse, left.astype(BF16)).astype(BF16)
        answer = mm(inverse, right.astype(BF16))
        solved_ref[at, :] = answer.astype(BF16)
        chained_ref[at, :] = answer


def chain_blocks(top_inverse, top_chain, top_blocks, top_rhs):
    tops, size, width = top_blocks.shape
    columns = top_rhs.shape[2]
    return pl.pallas_call(
        chain_kernel,
        out_shape=[
            jax.ShapeDtypeStruct((tops * size, width), BF16),
            jax.ShapeDtypeStruct((tops * size, columns), F32),
        ],
        scratch_shapes=[pltpu.VMEM((tops * size, columns), BF16)],
        compiler_params=params(),
        name="chain_blocks",
    )(top_inverse, top_chain, top_blocks, top_rhs)


def level_one_kernel(counts, rhs_ref, inverse_ref, mixed_ref, far_ref, *refs):
    parts, (out_ref, terms_ref, resid_ref) = refs[: sum(counts)], refs[sum(counts) :]
    half = parts[0].shape[0]
    first = 0
    for side, count in enumerate(counts):
        at = slice(side * half, (side + 1) * half)
        total = far_ref[at, :].astype(F32)
        for part in parts[first : first + count]:
            total += part[...].astype(F32)
        resid_ref[at, :] = (rhs_ref[at, :].astype(F32) - total).astype(BF16)
        first += count
    solved = mm(inverse_ref[...], resid_ref[...]).astype(BF16)
    out_ref[...] = solved
    terms_ref[...] = mm(mixed_ref[...], solved).astype(BF16)


def level_one(rhs, inverse, mixed, far, upper, lower):
    size, width = rhs.shape
    counts = (len(upper), len(lower))
    return pl.pallas_call(
        lambda *refs: level_one_kernel(counts, *refs),
        out_shape=[
            jax.ShapeDtypeStruct((size, width), BF16),
            jax.ShapeDtypeStruct((mixed.shape[0], width), BF16),
        ],
        scratch_shapes=[pltpu.VMEM((size, width), BF16)],
        compiler_params=params(),
        name="level_one",
    )(rhs, inverse, mixed, far, *upper, *lower)


def top_share(member, chained, terms):
    members, chunk, width = terms.shape
    own = lax.dynamic_slice_in_dim(chained, member * chunk, chunk, 0)
    share = (own - jnp.sum(terms.astype(F32), axis=0)).astype(BF16)
    return jnp.broadcast_to(share[None], (members, chunk, width))


def shards(
    rhs_in,
    rhs_target,
    leaf_inverse,
    level_one_blocks,
    level_one_pattern,
    level_one_rhs,
    level_one_inverse,
    top_blocks,
    top_rhs,
    top_inverse,
    top_chain,
):
    everyone = ("grid", "row", "col")
    device_count = lax.axis_size(everyone)
    rows, cols = lax.axis_size("row"), lax.axis_size("col")
    row, col = lax.axis_index("row"), lax.axis_index("col")
    team = ("grid", "row")

    def along(value, axis, step):
        size = lax.axis_size(axis)
        return lax.ppermute(value, axis, [(i, (i + step) % size) for i in range(size)])

    blocks, pattern = level_one_blocks[0, 0, 0], level_one_pattern[0, 0, 0].T
    after, before = pick(row, pattern, blocks, (1, rows - 1), SHORT)
    rhs_in, after, before = lax.optimization_barrier((rhs_in, after, before))
    after, before = along(after, "row", 1), along(before, "row", -1)
    send = route(rhs_target, rhs_in, device_count)
    local_rows, wide = send.shape
    got = lax.all_to_all(
        send.reshape(device_count, local_rows // device_count, wide),
        everyone,
        split_axis=0,
        concat_axis=0,
        tiled=True,
    ).reshape(local_rows, wide)
    mixed, chained_rhs = chain_blocks(top_inverse, top_chain, top_blocks[0, 0], top_rhs)
    after, before, blocks, mixed, chained_rhs = lax.optimization_barrier((after, before, blocks, mixed, chained_rhs))
    own, far = pick(row, pattern, blocks, (0, rows // 2), LONG)
    got, own, far = lax.optimization_barrier((got, own, far))
    far = along(far, "row", rows // 2)

    def over_cols(parts):
        return [parts[0]] + [along(part, "col", step) for step, part in enumerate(parts[1:], 1)]

    leaf_solution, upper, lower = leaf_near(col, cols, got, leaf_inverse, (own, after, before))
    upper = over_cols(upper)
    later, _ = lax.optimization_barrier((lower[2], far))
    lower = [lower[0], along(lower[1], "row", -1), along(later, "row", 1)]
    opposite = over_cols(couple_far(col, cols, leaf_solution, far))
    mine, to_last, to_next = part_sums(upper, True)
    upper = [mine, along(to_last, "row", -1), along(to_next, "row", 1)]
    lower = part_sums(lower, True)
    opposite, _ = lax.optimization_barrier((opposite, (lower[0], upper[1], upper[2])))
    lower = over_cols(lower)
    (to_far,) = part_sums(opposite, False, LONG)
    opposite = along(to_far, "row", rows // 2)

    solution_one, terms = level_one(level_one_rhs[0, 0], level_one_inverse[0, 0], mixed, opposite, upper, lower)
    members = lax.axis_size(team)
    terms = lax.all_to_all(
        terms.reshape(members, terms.shape[0] // members, terms.shape[1]), team, split_axis=0, concat_axis=0, tiled=True
    )
    share = top_share(lax.axis_index(team), chained_rhs, terms)
    top_solution = lax.all_to_all(share, team, split_axis=0, concat_axis=0, tiled=True)
    return (leaf_solution, solution_one[None, None], top_solution.reshape(top_rhs.shape))


def solution(mesh):
    in_specs = (
        P(("grid", "row", "col"), None),
        P(("grid", "row", "col")),
        P(("grid", "row", "col"), None, None),
        P("grid", "row", "col", None, None, None, None),
        P("grid", "row", "col", None, None),
        P("grid", "row", None, "col"),
        P("grid", "row", None, None),
        P("grid", "row", None, None, None),
        P(None, None, "col"),
        P(),
        P(),
    )
    out_specs = (
        P(("grid", "row", "col"), None),
        P("grid", "row", None, "col"),
        P(None, None, "col"),
    )
    return jax.shard_map(shards, mesh=mesh, in_specs=in_specs, out_specs=out_specs, check_vma=False)
```

```python
import jax
import jax.numpy as jnp
from jax import lax
from jax.experimental import pallas as pl
from jax.experimental.pallas import tpu as pltpu
from jax.sharding import PartitionSpec as P

F32 = jnp.float32
BF16 = jnp.bfloat16
LANES = 128
VMEM_LIMIT = 56 * 1024 * 1024
SHORT = pl.CostEstimate(flops=0, bytes_accessed=4 * 10**6, transcendentals=0)
LONG = pl.CostEstimate(flops=2 * 10**11, bytes_accessed=10**8, transcendentals=0)


def params():
    return pltpu.CompilerParams(vmem_limit_bytes=VMEM_LIMIT)


def mm(a, b):
    return jnp.dot(a, b, preferred_element_type=F32)


def mm_nt(a, b):
    return lax.dot_general(a, b, (((1,), (1,)), ((), ())), preferred_element_type=F32)


def pick_kernel(steps, row_ref, pattern_ref, block_ref, *outs):
    rows, leaves, size = pattern_ref.shape[1], block_ref.shape[1], block_ref.shape[2]
    for index, step in enumerate(steps):

        @pl.when(pl.program_id(0) == index)
        def _():
            for leaf in range(leaves):
                present = pattern_ref[leaf, (row_ref[0] + step) % rows].astype(F32).astype(BF16)
                outs[index][:, leaf * size : (leaf + 1) * size] = block_ref[0, leaf] * present


def pick(row, pattern, blocks, steps, cost):
    rows, leaves, size, _ = blocks.shape
    wide = (size, leaves * size)
    stride = steps[-1] - steps[0]
    return pl.pallas_call(
        lambda *refs: pick_kernel(steps, *refs),
        grid_spec=pltpu.PrefetchScalarGridSpec(
            num_scalar_prefetch=2,
            grid=(len(steps),),
            in_specs=[
                pl.BlockSpec(
                    (1, leaves, size, size),
                    lambda i, at, pattern: ((at[0] + steps[0] + stride * i) % rows, 0, 0, 0),
                )
            ],
            out_specs=[pl.BlockSpec(wide, lambda i, at, pattern: (0, 0))] * len(steps),
        ),
        out_shape=[jax.ShapeDtypeStruct(wide, BF16)] * len(steps),
        compiler_params=params(),
        cost_estimate=cost,
        name="pick",
    )(row.reshape(1), pattern, blocks)


def route_kernel(device_count, target_ref, rows_ref, out_ref, slot_ref):
    count = target_ref.shape[1]
    share = count // device_count
    part = out_ref.shape[0]
    width = rows_ref.shape[1]
    step = pl.program_id(0)

    @pl.when(step == 0)
    def _():
        target = target_ref[...]
        owner = target // count
        place = target % count
        piece = 2 * LANES
        before = (
            lax.broadcasted_iota(jnp.int32, (piece, piece), 0)
            < lax.broadcasted_iota(jnp.int32, (piece, piece), 1)
        ).astype(BF16)
        device = lax.broadcasted_iota(jnp.int32, (device_count, piece), 0)
        base = device[:, :1].astype(F32) * share
        for first in range(0, count, piece):
            mine = (device == owner[:, first : first + piece]).astype(F32)
            rank = mm(mine.astype(BF16), before) + base
            slot_ref[0:1, first : first + piece] = jnp.sum(mine * rank, axis=0, keepdims=True)
            base = base + jnp.sum(mine, axis=1, keepdims=True)
        slot_ref[1:2, :] = (place // 32).astype(F32)
        slot_ref[2:3, :] = (place % 32).astype(F32)

    slot = slot_ref[0:1, :].astype(jnp.int32)
    rows_at = lax.broadcasted_iota(jnp.int32, (part, count), 0) + step * part
    pick = (rows_at == slot).astype(BF16)
    out_ref[:, :width] = mm(pick, rows_ref[...]).astype(BF16)
    which = lax.broadcasted_iota(jnp.int32, (LANES, count), 0)
    digits = jnp.where(which == 0, slot_ref[1:2, :], jnp.where(which == 1, slot_ref[2:3, :], 0.0))
    out_ref[:, width:] = mm_nt(pick, digits.astype(BF16)).astype(BF16)


def route(rhs_target, rhs_in, device_count):
    rows, width = rhs_in.shape
    parts = 4
    return pl.pallas_call(
        lambda *refs: route_kernel(device_count, *refs),
        grid=(parts,),
        in_specs=[
            pl.BlockSpec((1, rows), lambda i: (0, 0)),
            pl.BlockSpec((rows, width), lambda i: (0, 0)),
        ],
        out_specs=pl.BlockSpec((rows // parts, width + LANES), lambda i: (i, 0)),
        out_shape=jax.ShapeDtypeStruct((rows, width + LANES), BF16),
        scratch_shapes=[pltpu.VMEM((8, rows), F32)],
        compiler_params=params(),
        name="route",
    )(rhs_target.reshape(1, rows), rhs_in)


def leaf_near_kernel(cols, at_ref, digits_ref, inverse_ref, got_ref, *refs):
    factors, solved_ref, outs, mixed_ref = refs[:3], refs[3], refs[4:-1], refs[-1]
    upper, lower = outs[:cols], outs[cols:]
    leaves, size = inverse_ref.shape[0], inverse_ref.shape[1]
    count, half = leaves * size, size // 2

    @pl.when(pl.program_id(0) == 0)
    def _():
        lane = lax.broadcasted_iota(jnp.int32, (8, LANES), 1)
        weights = jnp.where(lane == 0, 32.0, jnp.where(lane == 1, 1.0, 0.0)).astype(BF16)
        place = mm_nt(weights, digits_ref[...])[0:1, :].astype(jnp.int32)
        for leaf in range(leaves):
            at = slice(leaf * size, (leaf + 1) * size)
            rows_at = lax.broadcasted_iota(jnp.int32, (size, count), 0) + leaf * size
            pick_here = (rows_at == place).astype(BF16)
            mixed_ref[at, :] = mm(inverse_ref[leaf], pick_here).astype(BF16)

    solved_ref[...] = mm(mixed_ref[...], got_ref[...]).astype(BF16)
    for offset in range(cols):

        @pl.when(pl.program_id(0) == offset)
        def _():
            for index, factor in enumerate(factors):
                total = mm(factor[...], solved_ref[...])
                upper[offset][index] = total[:half].astype(BF16)
                lower[index][offset] = total[half:].astype(BF16)


def leaf_near(col, cols, got, leaf_inverse, factors):
    count = got.shape[0]
    width = got.shape[1] - LANES
    block = width // cols
    leaves, size, _ = leaf_inverse.shape
    near = len(factors)
    shapes = [(near, size // 2, block)] * cols + [(cols, size // 2, block)] * near
    outs = pl.pallas_call(
        lambda *refs: leaf_near_kernel(cols, *refs),
        grid_spec=pltpu.PrefetchScalarGridSpec(
            num_scalar_prefetch=1,
            grid=(cols,),
            in_specs=[
                pl.BlockSpec((count, LANES), lambda i, at: (0, width // LANES)),
                pl.BlockSpec((leaves, size, size), lambda i, at: (0, 0, 0)),
                pl.BlockSpec((count, block), lambda i, at: (0, (at[0] + i) % cols)),
            ]
            + [pl.BlockSpec((size, leaves * size), lambda i, at: (0, 0))] * near,
            out_specs=[pl.BlockSpec((count, block), lambda i, at: (0, (at[0] + i) % cols))]
            + [pl.BlockSpec(shape, lambda i, at: (0, 0, 0)) for shape in shapes],
            scratch_shapes=[pltpu.VMEM((count, count), BF16)],
        ),
        out_shape=[jax.ShapeDtypeStruct((count, width), BF16)] + [jax.ShapeDtypeStruct(shape, BF16) for shape in shapes],
        compiler_params=params(),
        name="leaf_near",
    )(col.reshape(1), got, leaf_inverse, got, *factors)
    return outs[0], outs[1 : 1 + cols], outs[1 + cols :]


def couple_far_kernel(cols, at_ref, solved_ref, factor_ref, *outs):
    for offset in range(cols):

        @pl.when(pl.program_id(0) == offset)
        def _():
            outs[offset][0] = mm(factor_ref[...], solved_ref[...]).astype(BF16)


def couple_far(col, cols, solved, factor):
    count, width = solved.shape
    block = width // cols
    shape = (1, factor.shape[0], block)
    return pl.pallas_call(
        lambda *refs: couple_far_kernel(cols, *refs),
        grid_spec=pltpu.PrefetchScalarGridSpec(
            num_scalar_prefetch=1,
            grid=(cols,),
            in_specs=[
                pl.BlockSpec((count, block), lambda i, at: (0, (at[0] + i) % cols)),
                pl.BlockSpec(factor.shape, lambda i, at: (0, 0)),
            ],
            out_specs=[pl.BlockSpec(shape, lambda i, at: (0, 0, 0))] * cols,
        ),
        out_shape=[jax.ShapeDtypeStruct(shape, BF16)] * cols,
        compiler_params=params(),
        cost_estimate=LONG,
        name="couple_far",
    )(col.reshape(1), solved, factor)


def part_sums_kernel(count, *refs):
    parts, outs = refs[:count], refs[count:]
    for index, out in enumerate(outs):
        total = parts[0][index].astype(F32)
        for part in parts[1:]:
            total += part[index].astype(F32)
        out[...] = total.astype(out.dtype)


def part_sums(parts, kept, cost=None):
    shape = parts[0].shape[1:]
    return pl.pallas_call(
        lambda *refs: part_sums_kernel(len(parts), *refs),
        out_shape=[
            jax.ShapeDtypeStruct(shape, F32 if index == 0 and kept else BF16) for index in range(parts[0].shape[0])
        ],
        compiler_params=params(),
        cost_estimate=cost,
        name="part_sums",
    )(*parts)


def chain_kernel(inverse_ref, chain_ref, blocks_ref, rhs_ref, mixed_ref, chained_ref, solved_ref):
    tops, size = inverse_ref.shape[0], inverse_ref.shape[1]
    for now in range(tops):
        left = blocks_ref[now].astype(F32)
        right = rhs_ref[now].astype(F32)
        for earlier in range(now):
            link = chain_ref[now * (now - 1) // 2 + earlier]
            at = slice(earlier * size, (earlier + 1) * size)
            left = left - mm(link, mixed_ref[at, :])
            right = right - mm(link, solved_ref[at, :])
        inverse = inverse_ref[now]
        at = slice(now * size, (now + 1) * size)
        mixed_ref[at, :] = mm(inverse, left.astype(BF16)).astype(BF16)
        answer = mm(inverse, right.astype(BF16))
        solved_ref[at, :] = answer.astype(BF16)
        chained_ref[at, :] = answer


def chain_blocks(top_inverse, top_chain, top_blocks, top_rhs):
    tops, size, width = top_blocks.shape
    columns = top_rhs.shape[2]
    return pl.pallas_call(
        chain_kernel,
        out_shape=[
            jax.ShapeDtypeStruct((tops * size, width), BF16),
            jax.ShapeDtypeStruct((tops * size, columns), F32),
        ],
        scratch_shapes=[pltpu.VMEM((tops * size, columns), BF16)],
        compiler_params=params(),
        name="chain_blocks",
    )(top_inverse, top_chain, top_blocks, top_rhs)


def level_one_kernel(counts, rhs_ref, inverse_ref, mixed_ref, far_ref, *refs):
    parts, (out_ref, terms_ref, resid_ref) = refs[: sum(counts)], refs[sum(counts) :]
    half = parts[0].shape[0]
    first = 0
    for side, count in enumerate(counts):
        at = slice(side * half, (side + 1) * half)
        total = far_ref[at, :].astype(F32)
        for part in parts[first : first + count]:
            total += part[...].astype(F32)
        resid_ref[at, :] = (rhs_ref[at, :].astype(F32) - total).astype(BF16)
        first += count
    solved = mm(inverse_ref[...], resid_ref[...]).astype(BF16)
    out_ref[...] = solved
    terms_ref[...] = mm(mixed_ref[...], solved).astype(BF16)


def level_one(rhs, inverse, mixed, far, upper, lower):
    size, width = rhs.shape
    counts = (len(upper), len(lower))
    return pl.pallas_call(
        lambda *refs: level_one_kernel(counts, *refs),
        out_shape=[
            jax.ShapeDtypeStruct((size, width), BF16),
            jax.ShapeDtypeStruct((mixed.shape[0], width), BF16),
        ],
        scratch_shapes=[pltpu.VMEM((size, width), BF16)],
        compiler_params=params(),
        name="level_one",
    )(rhs, inverse, mixed, far, *upper, *lower)


def top_share(member, chained, terms):
    members, chunk, width = terms.shape
    own = lax.dynamic_slice_in_dim(chained, member * chunk, chunk, 0)
    share = (own - jnp.sum(terms.astype(F32), axis=0)).astype(BF16)
    return jnp.broadcast_to(share[None], (members, chunk, width))


def shards(
    rhs_in,
    rhs_target,
    leaf_inverse,
    level_one_blocks,
    level_one_pattern,
    level_one_rhs,
    level_one_inverse,
    top_blocks,
    top_rhs,
    top_inverse,
    top_chain,
):
    everyone = ("grid", "row", "col")
    device_count = lax.axis_size(everyone)
    rows, cols = lax.axis_size("row"), lax.axis_size("col")
    row, col = lax.axis_index("row"), lax.axis_index("col")
    team = ("grid", "row")

    def along(value, axis, step):
        size = lax.axis_size(axis)
        return lax.ppermute(value, axis, [(i, (i + step) % size) for i in range(size)])

    blocks, pattern = level_one_blocks[0, 0, 0], level_one_pattern[0, 0, 0].T
    after, before = pick(row, pattern, blocks, (1, rows - 1), SHORT)
    rhs_in, after, before = lax.optimization_barrier((rhs_in, after, before))
    after, before = along(after, "row", 1), along(before, "row", -1)
    send = route(rhs_target, rhs_in, device_count)
    local_rows, wide = send.shape
    got = lax.all_to_all(
        send.reshape(device_count, local_rows // device_count, wide),
        everyone,
        split_axis=0,
        concat_axis=0,
        tiled=True,
    ).reshape(local_rows, wide)
    mixed, chained_rhs = chain_blocks(top_inverse, top_chain, top_blocks[0, 0], top_rhs)
    after, before, blocks, mixed, chained_rhs = lax.optimization_barrier((after, before, blocks, mixed, chained_rhs))
    own, far = pick(row, pattern, blocks, (0, rows // 2), LONG)
    got, own, far = lax.optimization_barrier((got, own, far))
    far = along(far, "row", rows // 2)

    def over_cols(parts):
        return [parts[0]] + [along(part, "col", step) for step, part in enumerate(parts[1:], 1)]

    leaf_solution, upper, lower = leaf_near(col, cols, got, leaf_inverse, (own, after, before))
    upper = over_cols(upper)
    later, _ = lax.optimization_barrier((lower[2], far))
    lower = [lower[0], along(lower[1], "row", -1), along(later, "row", 1)]
    opposite = over_cols(couple_far(col, cols, leaf_solution, far))
    mine, to_last, to_next = part_sums(upper, True)
    upper = [mine, along(to_last, "row", -1), along(to_next, "row", 1)]
    lower = part_sums(lower, True)
    opposite, _ = lax.optimization_barrier((opposite, (lower[0], upper[1], upper[2])))
    lower = over_cols(lower)
    to_far = sum(part[0].astype(F32) for part in opposite).astype(BF16)
    opposite = along(to_far, "row", rows // 2)

    solution_one, terms = level_one(level_one_rhs[0, 0], level_one_inverse[0, 0], mixed, opposite, upper, lower)
    members = lax.axis_size(team)
    terms = lax.all_to_all(
        terms.reshape(members, terms.shape[0] // members, terms.shape[1]), team, split_axis=0, concat_axis=0, tiled=True
    )
    share = top_share(lax.axis_index(team), chained_rhs, terms)
    top_solution = lax.all_to_all(share, team, split_axis=0, concat_axis=0, tiled=True)
    return (leaf_solution, solution_one[None, None], top_solution.reshape(top_rhs.shape))


def solution(mesh):
    in_specs = (
        P(("grid", "row", "col"), None),
        P(("grid", "row", "col")),
        P(("grid", "row", "col"), None, None),
        P("grid", "row", "col", None, None, None, None),
        P("grid", "row", "col", None, None),
        P("grid", "row", None, "col"),
        P("grid", "row", None, None),
        P("grid", "row", None, None, None),
        P(None, None, "col"),
        P(),
        P(),
    )
    out_specs = (
        P(("grid", "row", "col"), None),
        P("grid", "row", None, "col"),
        P(None, None, "col"),
    )
    return jax.shard_map(shards, mesh=mesh, in_specs=in_specs, out_specs=out_specs, check_vma=False)
```
